256 devices in a mesh: enc: 32 (over z_lo, x, core), seq: 8 (over z_hi, y).
Axes of the slice: x: 4, y: 4, z: 8 (z_hi: 2, z_lo: 4; z = z_hi * 4 + z_lo), core: 2. Of those that a mesh axis runs over, the one named last changes fastest.
Arguments:
- acts_clip: bfloat16 [8192, 1024], P('seq'), may hold values from -6 to 6
- acts_convnext: bfloat16 [8192, 3072], P('seq'), may hold values from -6 to 6
- acts_eva: bfloat16 [8192, 1024], P('seq'), may hold values from -6 to 6
- acts_sam: bfloat16 [8192, 1024], P('seq'), may hold values from -6 to 6
- cotangent: bfloat16 [8192, 5120], P('seq'), may hold values from -6 to 6
- weight_clip: bfloat16 [1024, 1024], P('seq', 'enc'), may hold values from -0.1875 to 0.1875
- weight_convnext: bfloat16 [3072, 3072], P('seq', 'enc'), may hold values from -0.109375 to 0.109375
- weight_eva: bfloat16 [1024, 1024], P('seq', 'enc'), may hold values from -0.1875 to 0.1875
- weight_sam: bfloat16 [1024, 1024], P('seq', 'enc'), may hold values from -0.1875 to 0.1875
- proj_clip: bfloat16 [5120, 1024], P('seq', 'enc'), may hold values from -0.078125 to 0.078125
- proj_convnext: bfloat16 [5120, 3072], P('seq', 'enc'), may hold values from -0.078125 to 0.078125
- proj_eva: bfloat16 [5120, 1024], P('seq', 'enc'), may hold values from -0.078125 to 0.078125
- proj_sam: bfloat16 [5120, 1024], P('seq', 'enc'), may hold values from -0.078125 to 0.078125
Outputs:
- grad_acts_clip: bfloat16 [8192, 1024], P('seq', 'enc')
- grad_acts_convnext: bfloat16 [8192, 3072], P('seq', 'enc')
- grad_acts_eva: bfloat16 [8192, 1024], P('seq', 'enc')
- grad_acts_sam: bfloat16 [8192, 1024], P('seq', 'enc')
- grad_weight_clip: float32 [1024, 1024], P('seq', 'enc')
- grad_weight_convnext: float32 [3072, 3072], P('seq', 'enc')
- grad_weight_eva: float32 [1024, 1024], P('seq', 'enc')
- grad_weight_sam: float32 [1024, 1024], P('seq', 'enc')
- grad_proj_clip: float32 [5120, 1024], P('seq', 'enc')
- grad_proj_convnext: float32 [5120, 3072], P('seq', 'enc')
- grad_proj_eva: float32 [5120, 1024], P('seq', 'enc')
- grad_proj_sam: float32 [5120, 1024], P('seq', 'enc')
The draws below stay inside these ranges and needn't reach their ends.
All inputs are finite; a program needn't handle non-finite values.
Results may differ from the reference program's by a relative error of at most 0.0035.
Values may be sent and summed in bfloat16 or wider, within the bound.
No kernel may reach another device: no remote copies, remote signals or barrier semaphores. Data moves between devices by JAX's collectives and lax.ppermute only.
A program may use at most 128 MiB of HBM per device.

```python
import jax
import jax.numpy as jnp
from jax import lax

E_CLIP = 1024
E_CONV = 3072
E_EVA = 1024
E_SAM = 1024
OUT = 5120
TOKENS = 8192
CONCAT = 6144


def steps_of(key, dims, cuts, least, top_value):
    def one(dim, shards_of):
        steps = jax.random.uniform(jax.random.fold_in(jax.random.fold_in(key, 6), dim), (shards_of,), jnp.float32, least / len(cuts), top_value / len(cuts))
        return jnp.repeat(jnp.exp(steps), dims[dim] // shards_of).reshape((-1,) + (1,) * (len(dims) - dim - 1))

    gain = one(*cuts[0])
    for cut in cuts[1:]:
        gain = gain * one(*cut)
    return gain


def noise(key, shape, scale, bound, split=(), kind=jnp.bfloat16):
    entries = jax.random.normal(key, shape, jnp.float32) * scale
    if len(split) > 0:
        entries = steps_of(key, shape, split, -0.22, 0.18) * entries
    return jnp.clip(entries, min=-bound, max=bound).astype(kind)


def setup_inputs(seed: int = 0) -> dict:
    streams_of = jax.random.split(jax.random.key(seed), 14)
    return {
        "acts_clip": noise(streams_of[0], (TOKENS, E_CLIP), 1.0, 6.0, ((0, 8),)),
        "acts_convnext": noise(streams_of[1], (TOKENS, E_CONV), 1.0, 6.0, ((0, 8),)),
        "acts_eva": noise(streams_of[2], (TOKENS, E_EVA), 1.0, 6.0, ((0, 8),)),
        "acts_sam": noise(streams_of[3], (TOKENS, E_SAM), 1.0, 6.0, ((0, 8),)),
        "cotangent": noise(streams_of[4], (TOKENS, OUT), 1.0, 6.0, ((0, 8),)),
        "weight_clip": noise(streams_of[5], (E_CLIP, E_CLIP), E_CLIP ** -0.5, 0.1875, ((0, 8), (1, 32))),
        "weight_convnext": noise(streams_of[6], (E_CONV, E_CONV), E_CONV ** -0.5, 0.109375, ((0, 8), (1, 32))),
        "weight_eva": noise(streams_of[7], (E_EVA, E_EVA), E_EVA ** -0.5, 0.1875, ((0, 8), (1, 32))),
        "weight_sam": noise(streams_of[8], (E_SAM, E_SAM), E_SAM ** -0.5, 0.1875, ((0, 8), (1, 32))),
        "proj_clip": noise(streams_of[9], (OUT, E_CLIP), CONCAT ** -0.5, 0.078125, ((0, 8), (1, 32))),
        "proj_convnext": noise(streams_of[10], (OUT, E_CONV), CONCAT ** -0.5, 0.078125, ((0, 8), (1, 32))),
        "proj_eva": noise(streams_of[11], (OUT, E_EVA), CONCAT ** -0.5, 0.078125, ((0, 8), (1, 32))),
        "proj_sam": noise(streams_of[12], (OUT, E_SAM), CONCAT ** -0.5, 0.078125, ((0, 8), (1, 32))),
    }


ROOT_HALF = 0.7071067811865476
INV_ROOT_TAU = 0.3989422804014327


def normal_cdf(values):
    return 0.5 * (1.0 + lax.erf(values * ROOT_HALF))


def slope_of(values):
    return normal_cdf(values) + values * jnp.exp(-0.5 * values * values) * INV_ROOT_TAU


def branch_grads(layer_input, weight, projection, cotangent, factor):
    pre_act = jnp.dot(layer_input, weight, preferred_element_type=jnp.float32)
    feature = (layer_input.astype(jnp.float32) + pre_act * normal_cdf(pre_act)).astype(jnp.bfloat16)
    back_grad = jnp.dot(cotangent, projection, preferred_element_type=jnp.float32)
    hidden_grad = (back_grad * slope_of(pre_act)).astype(jnp.bfloat16)
    input_grad = (back_grad + jnp.dot(hidden_grad, weight.T, preferred_element_type=jnp.float32)).astype(jnp.bfloat16)
    weight_grad = jnp.dot(layer_input.T, hidden_grad, preferred_element_type=jnp.float32) * factor
    proj_grad = jnp.dot(cotangent.T, feature, preferred_element_type=jnp.float32) * factor
    return input_grad, weight_grad, proj_grad


def reference(acts_clip, acts_convnext, acts_eva, acts_sam, cotangent, weight_clip, weight_convnext, weight_eva, weight_sam, proj_clip, proj_convnext, proj_eva, proj_sam):
    factor = float(TOKENS) ** -0.5
    first = branch_grads(acts_clip, weight_clip, proj_clip, cotangent, factor)
    second = branch_grads(acts_convnext, weight_convnext, proj_convnext, cotangent, factor)
    third = branch_grads(acts_eva, weight_eva, proj_eva, cotangent, factor)
    fourth = branch_grads(acts_sam, weight_sam, proj_sam, cotangent, factor)
    return (first[0], second[0], third[0], fourth[0], first[1], second[1], third[1], fourth[1], first[2], second[2], third[2], fourth[2])
```

```python
import jax
import jax.numpy as jnp
from jax import lax
from jax.sharding import Mesh, PartitionSpec as P

ROOT_HALF = 0.7071067811865476
INV_ROOT_TAU = 0.3989422804014327
LANES = 128
ENC = ("zl", "x", "core")
BF16 = jnp.bfloat16
F32 = jnp.float32


def normal_cdf(values):
    return 0.5 * (1.0 + lax.erf(values * ROOT_HALF))


def slope_of(values):
    return normal_cdf(values) + values * jnp.exp(-0.5 * values * values) * INV_ROOT_TAU


def dot(left, right, left_dim, right_dim):
    return lax.dot_general(
        left, right, (((left_dim,), (right_dim,)), ((), ())), preferred_element_type=F32
    )


def lane_chunks(block):
    cols, width = block.shape
    count = width // LANES
    return block.reshape(cols, count, LANES).transpose(1, 0, 2).reshape(count * cols, LANES)


def pack(blocks):
    return jnp.concatenate([lane_chunks(block.T) for block in blocks], axis=0)


def unpack(gathered, widths, counts):
    out = []
    start = 0
    for cols, count in zip(widths, counts):
        rows = cols * count
        piece = gathered[:, :, start : start + rows].reshape(4, 2, count, cols, LANES)
        out.append(piece.transpose(3, 1, 0, 2, 4).reshape(cols, 8 * count * LANES))
        start += rows
    return out


def spread(grads, counts):
    pieces = []
    for grad, count in zip(grads, counts):
        cols = grad.shape[0]
        piece = grad.reshape(cols, 2, 4, count, LANES).transpose(1, 2, 3, 0, 4)
        pieces.append(piece.reshape(2, 4, count * cols, LANES))
    return jnp.concatenate(pieces, axis=2)


def body(
    acts_clip,
    acts_convnext,
    acts_eva,
    acts_sam,
    cotangent,
    weight_clip,
    weight_convnext,
    weight_eva,
    weight_sam,
    proj_clip,
    proj_convnext,
    proj_eva,
    proj_sam,
):
    acts = (acts_clip, acts_convnext, acts_eva, acts_sam)
    zh = lax.axis_index("zh")
    enc = lax.axis_index(ENC)
    tokens = cotangent.shape[0]
    factor = float(8 * tokens) ** (-0.5)
    proj = jnp.concatenate([proj_clip, proj_convnext, proj_eva, proj_sam], axis=1)
    blocks = (weight_clip, weight_convnext, weight_eva, weight_sam, proj)
    widths = tuple(block.shape[1] for block in blocks)
    counts = tuple(block.shape[0] // LANES for block in blocks)
    swap = [(0, 1), (1, 0)]

    own = pack(blocks)
    other = lax.ppermute(own, "zh", swap)
    both = jnp.where(zh == 0, jnp.stack([own, other]), jnp.stack([other, own]))
    gathered = lax.all_gather(both, "y", axis=0)
    weight_t = unpack(gathered, widths, counts)
    proj_t = weight_t.pop()

    back_t = dot(proj_t, cotangent, 1, 1)
    pres = []
    owns = []
    for layer_input, weight in zip(acts, weight_t):
        cols = weight.shape[0]
        pres.append(dot(weight, layer_input, 1, 1))
        owns.append(lax.dynamic_slice_in_dim(layer_input, enc * cols, cols, 1).T)
    pre_t = jnp.concatenate(pres, axis=0)
    own_t = jnp.concatenate(owns, axis=0)
    feature_t = (own_t.astype(F32) + pre_t * normal_cdf(pre_t)).astype(BF16)
    hidden_t = (back_t * slope_of(pre_t)).astype(BF16)

    hidden_all = lax.all_gather(hidden_t, ENC, axis=0, tiled=True)

    narrow = jnp.concatenate([weight_t[0], weight_t[2], weight_t[3]], axis=0)
    small = widths[0]
    wide = widths[1]
    send = jnp.concatenate(
        [
            weight_t[1].reshape(wide, 32, wide).transpose(1, 0, 2),
            narrow.reshape(3 * small, 32, small).transpose(1, 0, 2),
        ],
        axis=2,
    )
    rows = lax.all_to_all(send, ENC, split_axis=0, concat_axis=0, tiled=True)

    def placed(block, left):
        return jnp.pad(block, ((0, 0), (0, 0), (left, sum(widths[:4]) - left - block.shape[2])))

    rows_t = jnp.concatenate(
        [
            placed(rows[:, :small, wide:], 0),
            placed(rows[:, :, :wide], small),
            placed(rows[:, small : 2 * small, wide:], small + wide),
            placed(rows[:, 2 * small :, wide:], 2 * small + wide),
        ],
        axis=1,
    ).reshape(hidden_all.shape[0], -1)

    grads = []
    start = 0
    for layer_input, cols in zip(acts, widths):
        grads.append(dot(hidden_t[start : start + cols], layer_input, 1, 0).astype(BF16))
        start += cols
    grads.append(dot(feature_t, cotangent, 1, 0).astype(BF16))
    parts = spread(grads, counts)
    parts = lax.all_to_all(parts, "y", split_axis=1, concat_axis=1, tiled=True)
    sums = jnp.sum(parts.astype(F32), axis=1)
    mine = lax.dynamic_index_in_dim(sums, zh, 0, keepdims=False)
    away = lax.dynamic_index_in_dim(sums, 1 - zh, 0, keepdims=False).astype(BF16)
    total = (mine + lax.ppermute(away, "zh", swap).astype(F32)) * factor
    finals = []
    start = 0
    for cols, count in zip(widths, counts):
        piece = total[start : start + cols * count].reshape(count, cols, LANES)
        finals.append(piece.transpose(0, 2, 1).reshape(count * LANES, cols))
        start += cols * count
    proj_grad = finals.pop()

    input_t = (back_t + dot(rows_t, hidden_all, 0, 0)).astype(BF16)
    bounds = []
    start = 0
    for cols in widths[:4]:
        bounds.append((start, start + cols))
        start += cols
    return (
        *[input_t[low:high].T for low, high in bounds],
        *finals,
        *[proj_grad[:, low:high] for low, high in bounds],
    )


def solution(mesh):
    split = Mesh(mesh.devices.reshape(4, 4, 2, 2, 4), ("zl", "x", "core", "zh", "y"))
    seq = ("zh", "y")
    whole = P(seq, None)
    tiled = P(seq, ENC)
    return jax.shard_map(
        body,
        mesh=split,
        in_specs=(whole,) * 5 + (tiled,) * 8,
        out_specs=(tiled,) * 12,
        check_vma=False,
    )
```

```python
import jax
import jax.numpy as jnp
from jax import lax
from jax.experimental import pallas as pl
from jax.experimental.pallas import tpu as pltpu
from jax.sharding import Mesh, PartitionSpec as P

ROOT_HALF = 0.7071067811865476
INV_ROOT_TAU = 0.3989422804014327
LANES = 128
ENC = ("zl", "x", "core")
BF16 = jnp.bfloat16
F32 = jnp.float32
SWAP = [(0, 1), (1, 0)]
SHIFTS = (1, 3, 2)
WIDE = 96
SMALL = 32
COLS = WIDE + 3 * SMALL
SPANS = ((0, 96), (96, 128), (128, 160), (160, 192))
W_ROWS = 3 * WIDE + 3 * SMALL
ROWS = W_ROWS + 5 * COLS
TILE = 256


def normal_cdf(values):
    return 0.5 * (1.0 + lax.erf(values * ROOT_HALF))


def slope_of(values):
    return normal_cdf(values) + values * jnp.exp(-0.5 * values * values) * INV_ROOT_TAU


def dot(left, right, left_dim, right_dim):
    return lax.dot_general(
        left, right, (((left_dim,), (right_dim,)), ((), ())), preferred_element_type=F32
    )


def lanes_of(start, width=LANES):
    return pl.ds(pl.multiple_of(start, LANES), width)


def pack_kernel(wv, wc, we, ws, pv, pc, pe, ps, out):
    for j in range(3):
        out[j * WIDE : (j + 1) * WIDE, :] = wv[:, j * LANES : (j + 1) * LANES]
    row = 3 * WIDE
    for ref in (wc, we, ws):
        out[row : row + SMALL, :] = ref[...]
        row += SMALL
    for ref, (low, high) in zip((pv, pc, pe, ps), SPANS):
        for j in range(5):
            at = W_ROWS + j * COLS
            out[at + low : at + high, :] = ref[:, j * LANES : (j + 1) * LANES]


def pack(*shards):
    return pl.pallas_call(
        pack_kernel,
        out_shape=jax.ShapeDtypeStruct((ROWS, LANES), BF16),
        name="pack",
    )(*shards)


def forward_kernel(place, *refs):
    gathered = refs[:8]
    acts = refs[8:12]
    cotangent, hidden, feature, back = refs[12:16]
    weights = refs[16:20]
    proj = refs[20]
    enc = place[8]

    @pl.when(pl.program_id(0) == 0)
    def _():
        for source, ref in enumerate(gathered):
            seq = place[source]
            for j in range(3):
                weights[0][:WIDE, lanes_of(seq * (3 * LANES) + j * LANES)] = ref[
                    j * WIDE : (j + 1) * WIDE, :
                ]
            row = 3 * WIDE
            for k in range(1, 4):
                weights[k][:SMALL, lanes_of(seq * LANES)] = ref[row : row + SMALL, :]
                row += SMALL
            for j in range(5):
                at = W_ROWS + j * COLS
                proj[:, lanes_of(seq * (5 * LANES) + j * LANES)] = ref[at : at + COLS, :]
        for k in range(4):
            cols = SPANS[k][1] - SPANS[k][0]
            shape = (cols, weights[k].shape[1])
            row = lax.broadcasted_iota(jnp.int32, shape, 0) + enc * cols
            lane = lax.broadcasted_iota(jnp.int32, shape, 1)
            weights[k][cols:, :] = jnp.where(row == lane, 1.0, 0.0).astype(BF16)

    back_t = dot(proj[...], cotangent[...], 1, 1)
    back[...] = back_t
    for k in range(4):
        low, high = SPANS[k]
        both = dot(weights[k][...], acts[k][...], 1, 1)
        pre = both[: high - low]
        cdf = normal_cdf(pre)
        slope = cdf + pre * jnp.exp(-0.5 * pre * pre) * INV_ROOT_TAU
        feature[low:high, :] = (both[high - low :] + pre * cdf).astype(BF16)
        hidden[low:high, :] = (back_t[low:high] * slope).astype(BF16)


def forward(place, gathered, acts, cotangent):
    tokens = cotangent.shape[0]
    whole = pl.BlockSpec((ROWS, LANES), lambda i, p: (0, 0))
    tall = lambda a: pl.BlockSpec((TILE, a.shape[1]), lambda i, p: (i, 0))
    flat = pl.BlockSpec((COLS, TILE), lambda i, p: (0, i))
    return pl.pallas_call(
        forward_kernel,
        grid_spec=pltpu.PrefetchScalarGridSpec(
            num_scalar_prefetch=1,
            grid=(tokens // TILE,),
            in_specs=[whole] * 8 + [tall(a) for a in acts] + [tall(cotangent)],
            out_specs=[flat] * 3,
            scratch_shapes=[
                pltpu.VMEM((2 * (high - low), a.shape[1]), BF16)
                for (low, high), a in zip(SPANS, acts)
            ]
            + [pltpu.VMEM((COLS, cotangent.shape[1]), BF16)],
        ),
        out_shape=[
            jax.ShapeDtypeStruct((COLS, tokens), BF16),
            jax.ShapeDtypeStruct((COLS, tokens), BF16),
            jax.ShapeDtypeStruct((COLS, tokens), F32),
        ],
        compiler_params=pltpu.CompilerParams(vmem_limit_bytes=50 * 2**20),
        name="forward",
    )(place, *gathered, *acts, cotangent)


def send_kernel(place, *refs):
    out = refs[8]
    for source, ref in enumerate(refs[:8]):
        seq = place[source]
        line = seq // 2
        first = (seq % 2) * 4
        wide = jnp.concatenate([ref[j * WIDE : (j + 1) * WIDE, :] for j in range(3)], axis=1)
        narrow = ref[3 * WIDE : W_ROWS, :]
        for j in range(4):
            out[first + j, line] = jnp.concatenate(
                [wide[:, j * WIDE : (j + 1) * WIDE], narrow[:, j * SMALL : (j + 1) * SMALL]],
                axis=1,
            )


def send_rows(place, gathered):
    return pl.pallas_call(
        send_kernel,
        grid_spec=pltpu.PrefetchScalarGridSpec(
            num_scalar_prefetch=1,
            grid=(1,),
            in_specs=[pl.BlockSpec((W_ROWS, LANES), lambda i, p: (0, 0))] * 8,
            out_specs=pl.BlockSpec((8, 4, WIDE, LANES), lambda i, p: (0, 0, 0, 0)),
        ),
        out_shape=jax.ShapeDtypeStruct((8, 4, WIDE, LANES), BF16),
        compiler_params=pltpu.CompilerParams(vmem_limit_bytes=32 * 2**20),
        name="send_rows",
    )(place, *gathered)


def expand_kernel(rows, out):
    lane = lax.broadcasted_iota(jnp.int32, (WIDE, LANES), 1)
    zero = jnp.zeros((WIDE, LANES), BF16)
    for group in range(4):
        pieces = []
        for j in range(2):
            block = rows[group * 2 + j, 0]
            conv = jnp.where(lane < WIDE, block, zero)
            rest = jnp.where(lane < WIDE, zero, block)
            clip = jnp.concatenate([rest[:SMALL], zero[:SMALL]], axis=1)
            turned = pltpu.roll(rest[SMALL:].astype(F32), SMALL, 1).astype(BF16)
            eva = jnp.concatenate([zero[:SMALL], turned[:SMALL]], axis=1)
            later = pltpu.roll(turned[SMALL:].astype(F32), SMALL, 1).astype(BF16)
            sam = jnp.concatenate([zero[:SMALL], later], axis=1)
            conv = jnp.concatenate([conv, zero], axis=1)
            pieces += [conv, clip, eva, sam]
        both = jnp.concatenate(pieces, axis=0)
        turned = both.astype(F32).T.astype(BF16)
        out[0, :, group * 2 * COLS : (group + 1) * 2 * COLS] = turned[:COLS]


def expand(rows):
    return pl.pallas_call(
        expand_kernel,
        grid=(4,),
        in_specs=[pl.BlockSpec((8, 1, WIDE, LANES), lambda i: (0, i, 0, 0))],
        out_specs=pl.BlockSpec((1, COLS, 8 * COLS), lambda i: (i, 0, 0)),
        out_shape=jax.ShapeDtypeStruct((4, COLS, 8 * COLS), BF16),
        name="expand_rows",
    )(rows)


def grads_kernel(hidden, feature, acts_v, acts_c, acts_e, acts_s, cotangent, out):
    wide = dot(hidden[:WIDE, :], acts_v[...], 1, 0).astype(BF16)
    for j in range(3):
        out[0, j * WIDE : (j + 1) * WIDE, :] = wide[:, j * LANES : (j + 1) * LANES]
    row = 3 * WIDE
    for (low, high), ref in zip(SPANS[1:], (acts_c, acts_e, acts_s)):
        out[0, row : row + SMALL, :] = dot(hidden[low:high, :], ref[...], 1, 0).astype(BF16)
        row += SMALL
    proj = dot(feature[...], cotangent[...], 1, 0).astype(BF16)
    for j in range(5):
        at = W_ROWS + j * COLS
        out[0, at : at + COLS, :] = proj[:, j * LANES : (j + 1) * LANES]


def grads(hidden, feature, acts, cotangent):
    tokens = cotangent.shape[0]
    whole = pl.BlockSpec((COLS, tokens), lambda i: (0, 0))
    part = lambda a: pl.BlockSpec((tokens, a.shape[1] // 8), lambda i: (0, i))
    return pl.pallas_call(
        grads_kernel,
        grid=(8,),
        in_specs=[whole] * 2 + [part(a) for a in acts] + [part(cotangent)],
        out_specs=pl.BlockSpec((1, ROWS, LANES), lambda i: ((i % 4) * 2 + i // 4, 0, 0)),
        out_shape=jax.ShapeDtypeStruct((8, ROWS, LANES), BF16),
        compiler_params=pltpu.CompilerParams(vmem_limit_bytes=50 * 2**20),
        name="grads",
    )(hidden, feature, *acts, cotangent)


def away_kernel(place, parts, out):
    total = parts[0, 0].astype(F32)
    for j in range(1, 4):
        total += parts[j, 0].astype(F32)
    out[...] = total.astype(BF16)


def away_sum(place, parts):
    return pl.pallas_call(
        away_kernel,
        grid_spec=pltpu.PrefetchScalarGridSpec(
            num_scalar_prefetch=1,
            grid=(1,),
            in_specs=[pl.BlockSpec((4, 1, ROWS, LANES), lambda i, p: (0, 1 - p[9], 0, 0))],
            out_specs=pl.BlockSpec((ROWS, LANES), lambda i, p: (0, 0)),
        ),
        out_shape=jax.ShapeDtypeStruct((ROWS, LANES), BF16),
        compiler_params=pltpu.CompilerParams(vmem_limit_bytes=32 * 2**20),
        name="away_sum",
    )(place, parts)


def unpack_kernel(factor, place, parts, other, wv, wc, we, ws, pv, pc, pe, ps):
    def total(low, high):
        rows = parts[0, 0, low:high].astype(F32)
        for j in range(1, 4):
            rows += parts[j, 0, low:high].astype(F32)
        return (rows + other[low:high].astype(F32)) * factor

    for j in range(3):
        wv[:, j * LANES : (j + 1) * LANES] = total(j * WIDE, (j + 1) * WIDE)
    row = 3 * WIDE
    for ref in (wc, we, ws):
        ref[...] = total(row, row + SMALL)
        row += SMALL
    for j in range(5):
        at = W_ROWS + j * COLS
        for ref, (low, high) in zip((pv, pc, pe, ps), SPANS):
            ref[:, j * LANES : (j + 1) * LANES] = total(at + low, at + high)


def unpack(place, parts, other, factor):
    sizes = [(WIDE, 384)] + [(SMALL, 128)] * 3 + [(WIDE, 640)] + [(SMALL, 640)] * 3
    return pl.pallas_call(
        lambda *refs: unpack_kernel(factor, *refs),
        grid_spec=pltpu.PrefetchScalarGridSpec(
            num_scalar_prefetch=1,
            grid=(1,),
            in_specs=[
                pl.BlockSpec((4, 1, ROWS, LANES), lambda i, p: (0, p[9], 0, 0)),
                pl.BlockSpec((ROWS, LANES), lambda i, p: (0, 0)),
            ],
            out_specs=[pl.BlockSpec(size, lambda i, p: (0, 0)) for size in sizes],
        ),
        out_shape=[jax.ShapeDtypeStruct(size, F32) for size in sizes],
        compiler_params=pltpu.CompilerParams(vmem_limit_bytes=32 * 2**20),
        name="unpack",
    )(place, parts, other)


def partial_kernel(rows, hidden, out):
    out[0] = dot(rows[0], hidden[...], 1, 0).astype(BF16)


def partial_inputs(rows, hidden):
    depth, tokens = hidden.shape
    return pl.pallas_call(
        partial_kernel,
        grid=(4,),
        in_specs=[
            pl.BlockSpec((1, COLS, depth), lambda i: (i, 0, 0)),
            pl.BlockSpec((depth, tokens), lambda i: (0, 0)),
        ],
        out_specs=pl.BlockSpec((1, COLS, tokens), lambda i: (i, 0, 0)),
        out_shape=jax.ShapeDtypeStruct((4, COLS, tokens), BF16),
        compiler_params=pltpu.CompilerParams(vmem_limit_bytes=32 * 2**20),
        name="partial_inputs",
    )(rows, hidden)


def finish_kernel(parts, back, *outs):
    for (low, high), ref in zip(SPANS, outs):
        total = parts[0, low:high].astype(F32)
        for j in range(1, 4):
            total += parts[j, low:high].astype(F32)
        ref[...] = (back[low:high, :] + total).astype(BF16)


def finish(parts, back):
    tokens = back.shape[1]
    return pl.pallas_call(
        finish_kernel,
        out_shape=[jax.ShapeDtypeStruct((high - low, tokens), BF16) for low, high in SPANS],
        compiler_params=pltpu.CompilerParams(vmem_limit_bytes=32 * 2**20),
        name="finish",
    )(parts, back)


def body(
    acts_clip,
    acts_convnext,
    acts_eva,
    acts_sam,
    cotangent,
    weight_clip,
    weight_convnext,
    weight_eva,
    weight_sam,
    proj_clip,
    proj_convnext,
    proj_eva,
    proj_sam,
):
    acts = (acts_convnext, acts_clip, acts_eva, acts_sam)
    zh = lax.axis_index("zh")
    y = lax.axis_index("y")
    enc = lax.axis_index(ENC)
    factor = float(8 * cotangent.shape[0]) ** (-0.5)

    def around(block):
        return [block] + [
            lax.ppermute(block, "y", [(i, (i + shift) % 4) for i in range(4)]) for shift in SHIFTS
        ]

    own = pack(
        weight_convnext.T,
        weight_clip.T,
        weight_eva.T,
        weight_sam.T,
        proj_convnext.T,
        proj_clip.T,
        proj_eva.T,
        proj_sam.T,
    )
    gathered = around(own) + around(lax.ppermute(own, "zh", SWAP))
    rows_from = [(y - shift) % 4 for shift in (0,) + SHIFTS]
    place = jnp.stack(
        [zh * 4 + r for r in rows_from] + [(1 - zh) * 4 + r for r in rows_from] + [enc, zh]
    ).astype(jnp.int32)

    hidden, feature, back = forward(place, gathered, acts, cotangent)
    inner = ("x", "core")
    hidden_all = lax.all_gather(hidden, inner, axis=0, tiled=True)

    rows = send_rows(place, gathered)
    rows, hidden, feature = lax.optimization_barrier((rows, hidden, feature))
    rows = expand(lax.all_to_all(rows, inner, split_axis=0, concat_axis=0, tiled=True))

    sums = grads(hidden, feature, acts, cotangent).reshape(4, 2, ROWS, LANES)
    sums = lax.all_to_all(sums, "y", split_axis=0, concat_axis=0, tiled=True)
    other = lax.ppermute(away_sum(place, sums), "zh", SWAP)

    parts = partial_inputs(rows, hidden_all)
    parts = lax.all_to_all(parts, "zl", split_axis=0, concat_axis=0, tiled=True)
    out_v, out_c, out_e, out_s = finish(parts, back)
    wv, wc, we, ws, pv, pc, pe, ps = unpack(place, sums, other, factor)
    outs = (out_c, out_v, out_e, out_s, wc, wv, we, ws, pc, pv, pe, ps)
    return tuple(out.T for out in outs)


def solution(mesh):
    split = Mesh(mesh.devices.reshape(4, 4, 2, 2, 4), ("zl", "x", "core", "zh", "y"))
    seq = ("zh", "y")
    whole = P(seq, None)
    tiled = P(seq, ENC)
    return jax.shard_map(
        body,
        mesh=split,
        in_specs=(whole,) * 5 + (tiled,) * 8,
        out_specs=(tiled,) * 12,
        check_vma=False,
    )
```

```python
import jax
import jax.numpy as jnp
from jax import lax
from jax.experimental import pallas as pl
from jax.experimental.pallas import tpu as pltpu
from jax.sharding import Mesh, PartitionSpec as P

ROOT_HALF = 0.7071067811865476
INV_ROOT_TAU = 0.3989422804014327
LANES = 128
ENC = ("zl", "x", "core")
BF16 = jnp.bfloat16
F32 = jnp.float32
SWAP = [(0, 1), (1, 0)]
SHIFTS = (1, 3, 2)
WIDE = 96
SMALL = 32
COLS = WIDE + 3 * SMALL
SPANS = ((0, 96), (96, 128), (128, 160), (160, 192))
W_ROWS = 3 * WIDE + 3 * SMALL
ROWS = W_ROWS + 5 * COLS
FIRST = 768
TILE = 256
VMEM = 20 * 2**20
MOST = 60 * 2**20


def normal_cdf(values):
    return 0.5 * (1.0 + lax.erf(values * ROOT_HALF))


def slope_of(values):
    return normal_cdf(values) + values * jnp.exp(-0.5 * values * values) * INV_ROOT_TAU


def dot(left, right, left_dim, right_dim):
    return lax.dot_general(
        left, right, (((left_dim,), (right_dim,)), ((), ())), preferred_element_type=F32
    )


def lanes_of(start, width=LANES):
    return pl.ds(pl.multiple_of(start, LANES), width)


def pack_kernel(wv, wc, we, ws, pv, pc, pe, ps, out):
    for j in range(3):
        out[j * WIDE : (j + 1) * WIDE, :] = wv[:, j * LANES : (j + 1) * LANES]
    row = 3 * WIDE
    for ref in (wc, we, ws):
        out[row : row + SMALL, :] = ref[...]
        row += SMALL
    for ref, (low, high) in zip((pv, pc, pe, ps), SPANS):
        for j in range(5):
            at = W_ROWS + j * COLS
            out[at + low : at + high, :] = ref[:, j * LANES : (j + 1) * LANES]


def pack(*shards):
    return pl.pallas_call(
        pack_kernel,
        out_shape=jax.ShapeDtypeStruct((ROWS, LANES), BF16),
        compiler_params=pltpu.CompilerParams(vmem_limit_bytes=MOST),
        name="pack",
    )(*shards)


def forward_kernel(place, *refs):
    gathered = refs[:8]
    acts = refs[8:12]
    cotangent, hidden, feature, back = refs[12:16]
    weights = refs[16:20]
    proj = refs[20]
    held = refs[21:26]
    arrived = refs[26]
    enc = place[8]
    tiles = cotangent.shape[0] // TILE
    copies = []
    for tile in range(tiles):
        at = slice(tile * TILE, (tile + 1) * TILE)
        for i, (source, target) in enumerate(zip((cotangent, *acts), held)):
            copy = pltpu.make_async_copy(source.at[at], target.at[at], arrived.at[tile, i])
            copy.start()
            copies.append(copy)

    for source, ref in enumerate(gathered):
        seq = place[source]
        for j in range(3):
            weights[0][:WIDE, lanes_of(seq * (3 * LANES) + j * LANES)] = ref[
                j * WIDE : (j + 1) * WIDE, :
            ]
        row = 3 * WIDE
        for k in range(1, 4):
            weights[k][:SMALL, lanes_of(seq * LANES)] = ref[row : row + SMALL, :]
            row += SMALL
        for j in range(5):
            at = W_ROWS + j * COLS
            proj[:, lanes_of(seq * (5 * LANES) + j * LANES)] = ref[at : at + COLS, :]
    for k in range(4):
        cols = SPANS[k][1] - SPANS[k][0]
        shape = (cols, weights[k].shape[1])
        row = lax.broadcasted_iota(jnp.int32, shape, 0) + enc * cols
        lane = lax.broadcasted_iota(jnp.int32, shape, 1)
        weights[k][cols:, :] = jnp.where(row == lane, 1.0, 0.0).astype(BF16)

    for tile in range(tiles):
        at = slice(tile * TILE, (tile + 1) * TILE)
        for copy in copies[tile * 5 : tile * 5 + 5]:
            copy.wait()
        back_t = dot(proj[...], held[0][at, :], 1, 1)
        back[:, at] = back_t
        for k in range(4):
            low, high = SPANS[k]
            both = dot(weights[k][...], held[1 + k][at, :], 1, 1)
            pre = both[: high - low]
            cdf = normal_cdf(pre)
            slope = cdf + pre * jnp.exp(-0.5 * pre * pre) * INV_ROOT_TAU
            feature[low:high, at] = (both[high - low :] + pre * cdf).astype(BF16)
            hidden[low:high, at] = (back_t[low:high] * slope).astype(BF16)


def forward(place, gathered, acts, cotangent):
    tokens = cotangent.shape[0]
    vmem = pl.BlockSpec(memory_space=pltpu.VMEM)
    return pl.pallas_call(
        forward_kernel,
        in_specs=[pl.BlockSpec(memory_space=pltpu.SMEM)] + [vmem] * 8
        + [pl.BlockSpec(memory_space=pl.ANY)] * 5,
        out_specs=[vmem] * 3,
        scratch_shapes=[
            pltpu.VMEM((2 * (high - low), a.shape[1]), BF16) for (low, high), a in zip(SPANS, acts)
        ]
        + [pltpu.VMEM((COLS, cotangent.shape[1]), BF16)]
        + [pltpu.VMEM(a.shape, BF16) for a in (cotangent, *acts)]
        + [pltpu.SemaphoreType.DMA((tokens // TILE, 5))],
        out_shape=[
            jax.ShapeDtypeStruct((COLS, tokens), BF16),
            jax.ShapeDtypeStruct((COLS, tokens), BF16),
            jax.ShapeDtypeStruct((COLS, tokens), F32),
        ],
        compiler_params=pltpu.CompilerParams(vmem_limit_bytes=MOST),
        name="forward",
    )(place, *gathered, *acts, cotangent)


def send_kernel(place, *refs):
    out = refs[8]
    for source, ref in enumerate(refs[:8]):
        seq = place[source]
        line = seq // 2
        first = (seq % 2) * 4
        wide = jnp.concatenate([ref[j * WIDE : (j + 1) * WIDE, :] for j in range(3)], axis=1)
        narrow = ref[3 * WIDE : W_ROWS, :]
        for j in range(4):
            out[first + j, line] = jnp.concatenate(
                [wide[:, j * WIDE : (j + 1) * WIDE], narrow[:, j * SMALL : (j + 1) * SMALL]],
                axis=1,
            )


def send_rows(place, gathered):
    return pl.pallas_call(
        send_kernel,
        grid_spec=pltpu.PrefetchScalarGridSpec(
            num_scalar_prefetch=1,
            grid=(1,),
            in_specs=[pl.BlockSpec((W_ROWS, LANES), lambda i, p: (0, 0))] * 8,
            out_specs=pl.BlockSpec((8, 4, WIDE, LANES), lambda i, p: (0, 0, 0, 0)),
        ),
        out_shape=jax.ShapeDtypeStruct((8, 4, WIDE, LANES), BF16),
        compiler_params=pltpu.CompilerParams(vmem_limit_bytes=VMEM),
        name="send_rows",
    )(place, *gathered)


def expand_kernel(rows, out):
    lane = lax.broadcasted_iota(jnp.int32, (WIDE, LANES), 1)
    zero = jnp.zeros((WIDE, LANES), BF16)
    for group in range(4):
        pieces = []
        for j in range(2):
            block = rows[group * 2 + j, 0]
            conv = jnp.where(lane < WIDE, block, zero)
            rest = jnp.where(lane < WIDE, zero, block)
            clip = jnp.concatenate([rest[:SMALL], zero[:SMALL]], axis=1)
            turned = pltpu.roll(rest[SMALL:].astype(F32), SMALL, 1).astype(BF16)
            eva = jnp.concatenate([zero[:SMALL], turned[:SMALL]], axis=1)
            later = pltpu.roll(turned[SMALL:].astype(F32), SMALL, 1).astype(BF16)
            sam = jnp.concatenate([zero[:SMALL], later], axis=1)
            conv = jnp.concatenate([conv, zero], axis=1)
            pieces += [conv, clip, eva, sam]
        both = jnp.concatenate(pieces, axis=0)
        turned = both.astype(F32).T.astype(BF16)
        out[0, :, group * 2 * COLS : (group + 1) * 2 * COLS] = turned[:COLS]


def expand(rows):
    return pl.pallas_call(
        expand_kernel,
        grid=(4,),
        in_specs=[pl.BlockSpec((8, 1, WIDE, LANES), lambda i: (0, i, 0, 0))],
        out_specs=pl.BlockSpec((1, COLS, 8 * COLS), lambda i: (i, 0, 0)),
        out_shape=jax.ShapeDtypeStruct((4, COLS, 8 * COLS), BF16),
        compiler_params=pltpu.CompilerParams(vmem_limit_bytes=VMEM),
        name="expand_rows",
    )(rows)


def grads_kernel(order, hidden, feature, *refs):
    sources = refs[:5]
    outs = refs[5:9]
    held = refs[9:14]
    arrived = refs[14]
    copies = []
    for step in range(4):
        for i, (source, target) in enumerate(zip(sources, held)):
            width = target.shape[2]
            copy = pltpu.make_async_copy(
                source.at[:, lanes_of(order[step] * width, width)],
                target.at[step],
                arrived.at[step, i],
            )
            copy.start()
            copies.append(copy)
    for step, out in enumerate(outs):
        for copy in copies[step * 5 : step * 5 + 5]:
            copy.wait()
        wide = dot(hidden[:WIDE, :], held[0][step], 1, 0)
        for j in range(3):
            out[j * WIDE : (j + 1) * WIDE, :] = wide[:, j * LANES : (j + 1) * LANES].astype(BF16)
        row = 3 * WIDE
        for (low, high), ref in zip(SPANS[1:], held[1:4]):
            out[row : row + SMALL, :] = dot(hidden[low:high, :], ref[step], 1, 0).astype(BF16)
            row += SMALL
        proj = dot(feature[...], held[4][step], 1, 0)
        for j in range(5):
            at = W_ROWS + j * COLS
            out[at : at + COLS, :] = proj[:, j * LANES : (j + 1) * LANES].astype(BF16)


def grads(order, hidden, feature, acts, cotangent):
    arrays = (*acts, cotangent)
    vmem = pl.BlockSpec(memory_space=pltpu.VMEM)
    return pl.pallas_call(
        grads_kernel,
        in_specs=[pl.BlockSpec(memory_space=pltpu.SMEM)]
        + [vmem] * 2
        + [pl.BlockSpec(memory_space=pl.ANY)] * 5,
        out_specs=[vmem] * 4,
        out_shape=[jax.ShapeDtypeStruct((ROWS, LANES), BF16)] * 4,
        scratch_shapes=[pltpu.VMEM((4, a.shape[0], a.shape[1] // 8), BF16) for a in arrays]
        + [pltpu.SemaphoreType.DMA((4, 5))],
        compiler_params=pltpu.CompilerParams(vmem_limit_bytes=MOST),
        name="grads",
    )(order, hidden, feature, *arrays)


def away_kernel(*refs):
    total = refs[0][...].astype(F32)
    for ref in refs[1:4]:
        total += ref[...].astype(F32)
    total = total.astype(BF16)
    refs[4][...] = total[:FIRST]
    refs[5][...] = total[FIRST:]


def away_sum(parts):
    return pl.pallas_call(
        away_kernel,
        out_shape=[
            jax.ShapeDtypeStruct((FIRST, LANES), BF16),
            jax.ShapeDtypeStruct((ROWS - FIRST, LANES), BF16),
        ],
        compiler_params=pltpu.CompilerParams(vmem_limit_bytes=VMEM),
        name="away_sum",
    )(*parts)


def unpack_kernel(factor, *refs):
    parts = refs[:4]
    first, second = refs[4:6]
    wv, wc, we, ws, pv, pc, pe, ps = refs[6:]

    def total(low, high):
        rows = parts[0][low:high].astype(F32)
        for ref in parts[1:]:
            rows += ref[low:high].astype(F32)
        if high <= FIRST:
            away = first[low:high]
        elif low >= FIRST:
            away = second[low - FIRST : high - FIRST]
        else:
            away = jnp.concatenate([first[low:FIRST], second[: high - FIRST]], axis=0)
        return (rows + away.astype(F32)) * factor

    for j in range(3):
        wv[:, j * LANES : (j + 1) * LANES] = total(j * WIDE, (j + 1) * WIDE)
    row = 3 * WIDE
    for ref in (wc, we, ws):
        ref[...] = total(row, row + SMALL)
        row += SMALL
    for j in range(5):
        at = W_ROWS + j * COLS
        for ref, (low, high) in zip((pv, pc, pe, ps), SPANS):
            ref[:, j * LANES : (j + 1) * LANES] = total(at + low, at + high)


def unpack(parts, factor):
    sizes = [(WIDE, 384)] + [(SMALL, 128)] * 3 + [(WIDE, 640)] + [(SMALL, 640)] * 3
    return pl.pallas_call(
        lambda *refs: unpack_kernel(factor, *refs),
        out_shape=[jax.ShapeDtypeStruct(size, F32) for size in sizes],
        compiler_params=pltpu.CompilerParams(vmem_limit_bytes=VMEM),
        name="unpack",
    )(*parts)


def partial_kernel(rows, hidden, out):
    out[0] = dot(rows[0], hidden[...], 1, 0).astype(BF16)


def partial_inputs(rows, hidden):
    depth, tokens = hidden.shape
    return pl.pallas_call(
        partial_kernel,
        grid=(4,),
        in_specs=[
            pl.BlockSpec((1, COLS, depth), lambda i: (i, 0, 0)),
            pl.BlockSpec((depth, tokens), lambda i: (0, 0)),
        ],
        out_specs=pl.BlockSpec((1, COLS, tokens), lambda i: (i, 0, 0)),
        out_shape=jax.ShapeDtypeStruct((4, COLS, tokens), BF16),
        compiler_params=pltpu.CompilerParams(vmem_limit_bytes=VMEM),
        name="partial_inputs",
    )(rows, hidden)


def finish_kernel(parts, back, *outs):
    for (low, high), ref in zip(SPANS, outs):
        total = parts[0, low:high].astype(F32)
        for j in range(1, 4):
            total += parts[j, low:high].astype(F32)
        ref[...] = (back[low:high, :] + total).astype(BF16)


def finish(parts, back):
    tokens = back.shape[1]
    return pl.pallas_call(
        finish_kernel,
        out_shape=[jax.ShapeDtypeStruct((high - low, tokens), BF16) for low, high in SPANS],
        compiler_params=pltpu.CompilerParams(vmem_limit_bytes=VMEM),
        name="finish",
    )(parts, back)


def body(
    acts_clip,
    acts_convnext,
    acts_eva,
    acts_sam,
    cotangent,
    weight_clip,
    weight_convnext,
    weight_eva,
    weight_sam,
    proj_clip,
    proj_convnext,
    proj_eva,
    proj_sam,
):
    acts = (acts_convnext, acts_clip, acts_eva, acts_sam)
    zh = lax.axis_index("zh")
    y = lax.axis_index("y")
    enc = lax.axis_index(ENC)
    factor = float(8 * cotangent.shape[0]) ** (-0.5)

    def turn(block, shift):
        return lax.ppermute(block, "y", [(i, (i + shift) % 4) for i in range(4)])

    def around(block):
        return [block] + [turn(block, shift) for shift in SHIFTS]

    own = pack(
        weight_convnext.T,
        weight_clip.T,
        weight_eva.T,
        weight_sam.T,
        proj_convnext.T,
        proj_clip.T,
        proj_eva.T,
        proj_sam.T,
    )
    gathered = around(own) + around(lax.ppermute(own, "zh", SWAP))
    rows_from = [(y - shift) & 3 for shift in (0,) + SHIFTS]
    place = jnp.stack(
        [zh * 4 + r for r in rows_from] + [(1 - zh) * 4 + r for r in rows_from] + [enc]
    ).astype(jnp.int32)

    hidden, feature, back = forward(place, gathered, acts, cotangent)
    inner = ("x", "core")
    hidden_all = lax.all_gather(hidden, inner, axis=0, tiled=True)

    heads = [(y + shift) & 3 for shift in (0,) + SHIFTS]

    def terms(half, hidden, feature):
        order = jnp.stack([half * 4 + head for head in heads]).astype(jnp.int32)
        return grads(order, hidden, feature, acts, cotangent)

    def turned(blocks):
        return [blocks[0]] + [turn(block, shift) for block, shift in zip(blocks[1:], SHIFTS)]

    away = terms(1 - zh, hidden, feature)
    away, hidden, feature, gathered = lax.optimization_barrier((away, hidden, feature, gathered))
    away = turned(away)
    rows = send_rows(place, gathered)
    rows, hidden, feature = lax.optimization_barrier((rows, hidden, feature))
    rows = lax.all_to_all(rows, inner, split_axis=0, concat_axis=0, tiled=True)
    near = terms(zh, hidden, feature)
    first, second = away_sum(away)
    first = lax.ppermute(first, "zh", SWAP)
    rows, near, first = lax.optimization_barrier((rows, near, first))
    rows = expand(rows)
    sums = turned(near) + [first, lax.ppermute(second, "zh", SWAP)]

    parts = partial_inputs(rows, hidden_all)
    parts = lax.all_to_all(parts, "zl", split_axis=0, concat_axis=0, tiled=True)
    out_v, out_c, out_e, out_s = finish(parts, back)
    wv, wc, we, ws, pv, pc, pe, ps = unpack(sums, factor)
    outs = (out_c, out_v, out_e, out_s, wc, wv, we, ws, pc, pv, pe, ps)
    return tuple(out.T for out in outs)


def solution(mesh):
    split = Mesh(mesh.devices.reshape(4, 4, 2, 2, 4), ("zl", "x", "core", "zh", "y"))
    seq = ("zh", "y")
    whole = P(seq, None)
    tiled = P(seq, ENC)
    return jax.shard_map(
        body,
        mesh=split,
        in_specs=(whole,) * 5 + (tiled,) * 8,
        out_specs=(tiled,) * 12,
        check_vma=False,
    )
```

```python
import jax
import jax.numpy as jnp
from jax import lax
from jax.experimental import pallas as pl
from jax.experimental.pallas import tpu as pltpu
from jax.sharding import Mesh, PartitionSpec as P

ROOT_HALF = 0.7071067811865476
INV_ROOT_TAU = 0.3989422804014327
LANES = 128
ENC = ("zl", "x", "core")
BF16 = jnp.bfloat16
F32 = jnp.float32
SWAP = [(0, 1), (1, 0)]
SHIFTS = (1, 3, 2)
WIDE = 96
SMALL = 32
COLS = WIDE + 3 * SMALL
SPANS = ((0, 96), (96, 128), (128, 160), (160, 192))
W_ROWS = 3 * WIDE + 3 * SMALL
ROWS = W_ROWS + 5 * COLS
TILE = 256
VMEM = 20 * 2**20
MOST = 60 * 2**20


def normal_cdf(values):
    return 0.5 * (1.0 + lax.erf(values * ROOT_HALF))


def slope_of(values):
    return normal_cdf(values) + values * jnp.exp(-0.5 * values * values) * INV_ROOT_TAU


def dot(left, right, left_dim, right_dim):
    return lax.dot_general(
        left, right, (((left_dim,), (right_dim,)), ((), ())), preferred_element_type=F32
    )


def lanes_of(start, width=LANES):
    return pl.ds(pl.multiple_of(start, LANES), width)


def pack_kernel(wv, wc, we, ws, pv, pc, pe, ps, out):
    for j in range(3):
        out[j * WIDE : (j + 1) * WIDE, :] = wv[:, j * LANES : (j + 1) * LANES]
    row = 3 * WIDE
    for ref in (wc, we, ws):
        out[row : row + SMALL, :] = ref[...]
        row += SMALL
    for ref, (low, high) in zip((pv, pc, pe, ps), SPANS):
        for j in range(5):
            at = W_ROWS + j * COLS
            out[at + low : at + high, :] = ref[:, j * LANES : (j + 1) * LANES]


def pack(*shards):
    return pl.pallas_call(
        pack_kernel,
        out_shape=jax.ShapeDtypeStruct((ROWS, LANES), BF16),
        compiler_params=pltpu.CompilerParams(vmem_limit_bytes=MOST),
        name="pack",
    )(*shards)


def forward_kernel(place, *refs):
    gathered = refs[:8]
    acts = refs[8:12]
    cotangent, hidden, feature, back = refs[12:16]
    weights = refs[16:20]
    proj = refs[20]
    held = refs[21:26]
    arrived = refs[26]
    enc = place[8]
    tiles = cotangent.shape[0] // TILE
    copies = []
    for tile in range(tiles):
        at = slice(tile * TILE, (tile + 1) * TILE)
        for i, (source, target) in enumerate(zip((cotangent, *acts), held)):
            copy = pltpu.make_async_copy(source.at[at], target.at[at], arrived.at[tile, i])
            copy.start()
            copies.append(copy)

    for source, ref in enumerate(gathered):
        seq = place[source]
        for j in range(3):
            weights[0][:WIDE, lanes_of(seq * (3 * LANES) + j * LANES)] = ref[
                j * WIDE : (j + 1) * WIDE, :
            ]
        row = 3 * WIDE
        for k in range(1, 4):
            weights[k][:SMALL, lanes_of(seq * LANES)] = ref[row : row + SMALL, :]
            row += SMALL
        for j in range(5):
            at = W_ROWS + j * COLS
            proj[:, lanes_of(seq * (5 * LANES) + j * LANES)] = ref[at : at + COLS, :]
    for k in range(4):
        cols = SPANS[k][1] - SPANS[k][0]
        shape = (cols, weights[k].shape[1])
        row = lax.broadcasted_iota(jnp.int32, shape, 0) + enc * cols
        lane = lax.broadcasted_iota(jnp.int32, shape, 1)
        weights[k][cols:, :] = jnp.where(row == lane, 1.0, 0.0).astype(BF16)

    for tile in range(tiles):
        at = slice(tile * TILE, (tile + 1) * TILE)
        for copy in copies[tile * 5 : tile * 5 + 5]:
            copy.wait()
        back_t = dot(proj[...], held[0][at, :], 1, 1)
        back[:, at] = back_t
        for k in range(4):
            low, high = SPANS[k]
            both = dot(weights[k][...], held[1 + k][at, :], 1, 1)
            pre = both[: high - low]
            cdf = normal_cdf(pre)
            slope = cdf + pre * jnp.exp(-0.5 * pre * pre) * INV_ROOT_TAU
            feature[low:high, at] = (both[high - low :] + pre * cdf).astype(BF16)
            hidden[low:high, at] = (back_t[low:high] * slope).astype(BF16)


def forward(place, gathered, acts, cotangent):
    tokens = cotangent.shape[0]
    vmem = pl.BlockSpec(memory_space=pltpu.VMEM)
    return pl.pallas_call(
        forward_kernel,
        in_specs=[pl.BlockSpec(memory_space=pltpu.SMEM)] + [vmem] * 8
        + [pl.BlockSpec(memory_space=pl.ANY)] * 5,
        out_specs=[vmem] * 3,
        scratch_shapes=[
            pltpu.VMEM((2 * (high - low), a.shape[1]), BF16) for (low, high), a in zip(SPANS, acts)
        ]
        + [pltpu.VMEM((COLS, cotangent.shape[1]), BF16)]
        + [pltpu.VMEM(a.shape, BF16) for a in (cotangent, *acts)]
        + [pltpu.SemaphoreType.DMA((tokens // TILE, 5))],
        out_shape=[
            jax.ShapeDtypeStruct((COLS, tokens), BF16),
            jax.ShapeDtypeStruct((COLS, tokens), BF16),
            jax.ShapeDtypeStruct((COLS, tokens), F32),
        ],
        compiler_params=pltpu.CompilerParams(vmem_limit_bytes=MOST),
        name="forward",
    )(place, *gathered, *acts, cotangent)


def send_kernel(place, *refs):
    out = refs[8]
    for source, ref in enumerate(refs[:8]):
        seq = place[source]
        line = seq // 2
        first = (seq % 2) * 4
        wide = jnp.concatenate([ref[j * WIDE : (j + 1) * WIDE, :] for j in range(3)], axis=1)
        narrow = ref[3 * WIDE : W_ROWS, :]
        for j in range(4):
            out[first + j, line] = jnp.concatenate(
                [wide[:, j * WIDE : (j + 1) * WIDE], narrow[:, j * SMALL : (j + 1) * SMALL]],
                axis=1,
            )


def send_rows(place, gathered):
    return pl.pallas_call(
        send_kernel,
        grid_spec=pltpu.PrefetchScalarGridSpec(
            num_scalar_prefetch=1,
            grid=(1,),
            in_specs=[pl.BlockSpec((W_ROWS, LANES), lambda i, p: (0, 0))] * 8,
            out_specs=pl.BlockSpec((8, 4, WIDE, LANES), lambda i, p: (0, 0, 0, 0)),
        ),
        out_shape=jax.ShapeDtypeStruct((8, 4, WIDE, LANES), BF16),
        compiler_params=pltpu.CompilerParams(vmem_limit_bytes=VMEM),
        name="send_rows",
    )(place, *gathered)


def expand_kernel(order, rows, out):
    lane = lax.broadcasted_iota(jnp.int32, (WIDE, LANES), 1)
    zero = jnp.zeros((WIDE, LANES), BF16)
    for group in range(4):
        pieces = []
        for j in range(2):
            block = rows[order[4 + group * 2 + j], 0]
            conv = jnp.where(lane < WIDE, block, zero)
            rest = jnp.where(lane < WIDE, zero, block)
            clip = jnp.concatenate([rest[:SMALL], zero[:SMALL]], axis=1)
            turned = pltpu.roll(rest[SMALL:].astype(F32), SMALL, 1).astype(BF16)
            eva = jnp.concatenate([zero[:SMALL], turned[:SMALL]], axis=1)
            later = pltpu.roll(turned[SMALL:].astype(F32), SMALL, 1).astype(BF16)
            sam = jnp.concatenate([zero[:SMALL], later], axis=1)
            conv = jnp.concatenate([conv, zero], axis=1)
            pieces += [conv, clip, eva, sam]
        both = jnp.concatenate(pieces, axis=0)
        turned = both.astype(F32).T.astype(BF16)
        out[0, :, group * 2 * COLS : (group + 1) * 2 * COLS] = turned[:COLS]


def expand(order, rows):
    return pl.pallas_call(
        expand_kernel,
        grid_spec=pltpu.PrefetchScalarGridSpec(
            num_scalar_prefetch=1,
            grid=(4,),
            in_specs=[pl.BlockSpec((8, 1, WIDE, LANES), lambda i, p: (0, p[i], 0, 0))],
            out_specs=pl.BlockSpec((1, COLS, 8 * COLS), lambda i, p: (i, 0, 0)),
        ),
        out_shape=jax.ShapeDtypeStruct((4, COLS, 8 * COLS), BF16),
        compiler_params=pltpu.CompilerParams(vmem_limit_bytes=VMEM),
        name="expand_rows",
    )(order, rows)


def grads_kernel(order, hidden, feature, *refs):
    sources = refs[:5]
    outs = refs[5:9]
    held = refs[9:14]
    arrived = refs[14]
    copies = []
    for step in range(4):
        for i, (source, target) in enumerate(zip(sources, held)):
            width = target.shape[2]
            copy = pltpu.make_async_copy(
                source.at[:, lanes_of(order[step] * width, width)],
                target.at[step],
                arrived.at[step, i],
            )
            copy.start()
            copies.append(copy)
    for step, out in enumerate(outs):
        for copy in copies[step * 5 : step * 5 + 5]:
            copy.wait()
        wide = dot(hidden[:WIDE, :], held[0][step], 1, 0)
        for j in range(3):
            out[j * WIDE : (j + 1) * WIDE, :] = wide[:, j * LANES : (j + 1) * LANES].astype(BF16)
        row = 3 * WIDE
        for (low, high), ref in zip(SPANS[1:], held[1:4]):
            out[row : row + SMALL, :] = dot(hidden[low:high, :], ref[step], 1, 0).astype(BF16)
            row += SMALL
        proj = dot(feature[...], held[4][step], 1, 0)
        for j in range(5):
            at = W_ROWS + j * COLS
            out[at : at + COLS, :] = proj[:, j * LANES : (j + 1) * LANES].astype(BF16)


def grads(order, hidden, feature, acts, cotangent):
    arrays = (*acts, cotangent)
    vmem = pl.BlockSpec(memory_space=pltpu.VMEM)
    return pl.pallas_call(
        grads_kernel,
        in_specs=[pl.BlockSpec(memory_space=pltpu.SMEM)]
        + [vmem] * 2
        + [pl.BlockSpec(memory_space=pl.ANY)] * 5,
        out_specs=[vmem] * 4,
        out_shape=[jax.ShapeDtypeStruct((ROWS, LANES), BF16)] * 4,
        scratch_shapes=[pltpu.VMEM((4, a.shape[0], a.shape[1] // 8), BF16) for a in arrays]
        + [pltpu.SemaphoreType.DMA((4, 5))],
        compiler_params=pltpu.CompilerParams(vmem_limit_bytes=MOST),
        name="grads",
    )(order, hidden, feature, *arrays)


def away_kernel(*refs):
    total = refs[0][...].astype(F32)
    for ref in refs[1:4]:
        total += ref[...].astype(F32)
    refs[4][...] = total.astype(BF16)


def away_sum(parts):
    return pl.pallas_call(
        away_kernel,
        out_shape=jax.ShapeDtypeStruct((ROWS, LANES), BF16),
        compiler_params=pltpu.CompilerParams(vmem_limit_bytes=VMEM),
        name="away_sum",
    )(*parts)


def unpack_kernel(factor, *refs):
    parts = refs[:5]
    wv, wc, we, ws, pv, pc, pe, ps = refs[5:]

    def total(low, high):
        rows = parts[0][low:high].astype(F32)
        for ref in parts[1:]:
            rows += ref[low:high].astype(F32)
        return rows * factor

    for j in range(3):
        wv[:, j * LANES : (j + 1) * LANES] = total(j * WIDE, (j + 1) * WIDE)
    row = 3 * WIDE
    for ref in (wc, we, ws):
        ref[...] = total(row, row + SMALL)
        row += SMALL
    for j in range(5):
        at = W_ROWS + j * COLS
        for ref, (low, high) in zip((pv, pc, pe, ps), SPANS):
            ref[:, j * LANES : (j + 1) * LANES] = total(at + low, at + high)


def unpack(parts, factor):
    sizes = [(WIDE, 384)] + [(SMALL, 128)] * 3 + [(WIDE, 640)] + [(SMALL, 640)] * 3
    return pl.pallas_call(
        lambda *refs: unpack_kernel(factor, *refs),
        out_shape=[jax.ShapeDtypeStruct(size, F32) for size in sizes],
        compiler_params=pltpu.CompilerParams(vmem_limit_bytes=VMEM),
        name="unpack",
    )(*parts)


def partial_kernel(rows, *refs):
    outs, whole = refs[8:12], refs[12]

    @pl.when(pl.program_id(0) == 0)
    def _():
        for j, ref in enumerate(refs[:8]):
            whole[j * COLS : (j + 1) * COLS, :] = ref[...]

    part = dot(rows[0], whole[...], 1, 0).astype(BF16)
    for step, out in enumerate(outs):

        @pl.when(pl.program_id(0) == step)
        def _(out=out):
            out[...] = part


def partial_inputs(rows, hidden):
    tokens = hidden[0].shape[1]
    block = pl.BlockSpec((COLS, tokens), lambda i: (0, 0))
    return pl.pallas_call(
        partial_kernel,
        grid=(4,),
        in_specs=[pl.BlockSpec((1, COLS, 8 * COLS), lambda i: (i, 0, 0))] + [block] * 8,
        out_specs=[block] * 4,
        out_shape=[jax.ShapeDtypeStruct((COLS, tokens), BF16)] * 4,
        scratch_shapes=[pltpu.VMEM((8 * COLS, tokens), BF16)],
        compiler_params=pltpu.CompilerParams(vmem_limit_bytes=VMEM),
        name="partial_inputs",
    )(rows, *hidden)


def finish_kernel(back, *refs):
    for (low, high), out in zip(SPANS, refs[4:]):
        total = refs[0][low:high].astype(F32)
        for ref in refs[1:4]:
            total += ref[low:high].astype(F32)
        out[...] = (back[low:high, :] + total).astype(BF16)


def finish(parts, back):
    tokens = back.shape[1]
    return pl.pallas_call(
        finish_kernel,
        out_shape=[jax.ShapeDtypeStruct((high - low, tokens), BF16) for low, high in SPANS],
        compiler_params=pltpu.CompilerParams(vmem_limit_bytes=VMEM),
        name="finish",
    )(back, *parts)


def body(
    acts_clip,
    acts_convnext,
    acts_eva,
    acts_sam,
    cotangent,
    weight_clip,
    weight_convnext,
    weight_eva,
    weight_sam,
    proj_clip,
    proj_convnext,
    proj_eva,
    proj_sam,
):
    acts = (acts_convnext, acts_clip, acts_eva, acts_sam)
    zh = lax.axis_index("zh")
    y = lax.axis_index("y")
    enc = lax.axis_index(ENC)
    factor = float(8 * cotangent.shape[0]) ** (-0.5)

    def turn(block, shift, axis="y"):
        return lax.ppermute(block, axis, [(i, (i + shift) % 4) for i in range(4)])

    def around(block, axis="y"):
        return [block] + [turn(block, shift, axis) for shift in SHIFTS]

    def turned(blocks, axis="y"):
        return [blocks[0]] + [turn(b, shift, axis) for b, shift in zip(blocks[1:], SHIFTS)]

    own = pack(
        weight_convnext.T,
        weight_clip.T,
        weight_eva.T,
        weight_sam.T,
        proj_convnext.T,
        proj_clip.T,
        proj_eva.T,
        proj_sam.T,
    )
    gathered = around(own) + around(lax.ppermute(own, "zh", SWAP))
    rows_from = [(y - shift) & 3 for shift in (0,) + SHIFTS]
    place = jnp.stack(
        [zh * 4 + r for r in rows_from] + [(1 - zh) * 4 + r for r in rows_from] + [enc]
    ).astype(jnp.int32)

    heads = [(y + shift) & 3 for shift in (0,) + SHIFTS]
    order_away = jnp.stack([(1 - zh) * 4 + head for head in heads]).astype(jnp.int32)
    order_near = jnp.stack([zh * 4 + head for head in heads]).astype(jnp.int32)
    zl = lax.axis_index("zl")
    core = lax.axis_index("core")
    x_from = [((lax.axis_index("x") - shift) & 3) * 2 for shift in (0,) + SHIFTS]
    order_rows = jnp.stack(
        [(zl + shift) & 3 for shift in (0,) + SHIFTS]
        + [x + core for x in x_from]
        + [x + 1 - core for x in x_from]
    ).astype(jnp.int32)

    rows = send_rows(place, gathered)
    rows, gathered = lax.optimization_barrier((rows, gathered))
    rows = lax.all_to_all(rows, ("x", "core"), split_axis=0, concat_axis=0, tiled=True)

    hidden, feature, back = forward(place, gathered, acts, cotangent)
    hidden_all = around(hidden, "x")
    hidden_all = hidden_all + [lax.ppermute(block, "core", SWAP) for block in hidden_all]

    away = turned(grads(order_away, hidden, feature, acts, cotangent))
    other = lax.ppermute(away_sum(away), "zh", SWAP)

    parts = partial_inputs(expand(order_rows, rows), hidden_all)
    parts, hidden, feature = lax.optimization_barrier((parts, hidden, feature))
    sums = turned(grads(order_near, hidden, feature, acts, cotangent)) + [other]
    parts = turned(parts, "zl")
    out_v, out_c, out_e, out_s = finish(parts, back)
    wv, wc, we, ws, pv, pc, pe, ps = unpack(sums, factor)
    outs = (out_c, out_v, out_e, out_s, wc, wv, we, ws, pc, pv, pe, ps)
    return tuple(out.T for out in outs)


def solution(mesh):
    split = Mesh(mesh.devices.reshape(4, 4, 2, 2, 4), ("zl", "x", "core", "zh", "y"))
    seq = ("zh", "y")
    whole = P(seq, None)
    tiled = P(seq, ENC)
    return jax.shard_map(
        body,
        mesh=split,
        in_specs=(whole,) * 5 + (tiled,) * 8,
        out_specs=(tiled,) * 12,
        check_vma=False,
    )
```

```python
import jax
import jax.numpy as jnp
from jax import lax
from jax.experimental import pallas as pl
from jax.experimental.pallas import tpu as pltpu
from jax.sharding import Mesh, PartitionSpec as P

ROOT_HALF = 0.7071067811865476
INV_ROOT_TAU = 0.3989422804014327
LANES = 128
ENC = ("zl", "x", "core")
BF16 = jnp.bfloat16
F32 = jnp.float32
SWAP = [(0, 1), (1, 0)]
SHIFTS = (1, 3, 2)
WIDE = 96
SMALL = 32
COLS = WIDE + 3 * SMALL
SPANS = ((0, 96), (96, 128), (128, 160), (160, 192))
W_ROWS = 3 * WIDE + 3 * SMALL
ROWS = W_ROWS + 5 * COLS
TILE = 256
VMEM = 20 * 2**20
MOST = 60 * 2**20


def normal_cdf(values):
    return 0.5 * (1.0 + lax.erf(values * ROOT_HALF))


def slope_of(values):
    return normal_cdf(values) + values * jnp.exp(-0.5 * values * values) * INV_ROOT_TAU


def dot(left, right, left_dim, right_dim):
    return lax.dot_general(
        left, right, (((left_dim,), (right_dim,)), ((), ())), preferred_element_type=F32
    )


def lanes_of(start, width=LANES):
    return pl.ds(pl.multiple_of(start, LANES), width)


def pack_kernel(wv, wc, we, ws, pv, pc, pe, ps, out):
    for j in range(3):
        out[j * WIDE : (j + 1) * WIDE, :] = wv[:, j * LANES : (j + 1) * LANES]
    row = 3 * WIDE
    for ref in (wc, we, ws):
        out[row : row + SMALL, :] = ref[...]
        row += SMALL
    for ref, (low, high) in zip((pv, pc, pe, ps), SPANS):
        for j in range(5):
            at = W_ROWS + j * COLS
            out[at + low : at + high, :] = ref[:, j * LANES : (j + 1) * LANES]


def pack(*shards):
    return pl.pallas_call(
        pack_kernel,
        out_shape=jax.ShapeDtypeStruct((ROWS, LANES), BF16),
        compiler_params=pltpu.CompilerParams(vmem_limit_bytes=MOST),
        name="pack",
    )(*shards)


def forward_kernel(place, *refs):
    gathered = refs[:8]
    acts = refs[8:12]
    cotangent, hidden, feature, back = refs[12:16]
    weights = refs[16:20]
    proj = refs[20]
    held = refs[21:26]
    arrived = refs[26]
    enc = place[8]
    tiles = cotangent.shape[0] // TILE
    copies = []
    for tile in range(tiles):
        at = slice(tile * TILE, (tile + 1) * TILE)
        for i, (source, target) in enumerate(zip((cotangent, *acts), held)):
            copy = pltpu.make_async_copy(source.at[at], target.at[at], arrived.at[tile, i])
            copy.start()
            copies.append(copy)

    for source, ref in enumerate(gathered):
        seq = place[source]
        for j in range(3):
            weights[0][:WIDE, lanes_of(seq * (3 * LANES) + j * LANES)] = ref[
                j * WIDE : (j + 1) * WIDE, :
            ]
        row = 3 * WIDE
        for k in range(1, 4):
            weights[k][:SMALL, lanes_of(seq * LANES)] = ref[row : row + SMALL, :]
            row += SMALL
        for j in range(5):
            at = W_ROWS + j * COLS
            proj[:, lanes_of(seq * (5 * LANES) + j * LANES)] = ref[at : at + COLS, :]
    for k in range(4):
        cols = SPANS[k][1] - SPANS[k][0]
        shape = (cols, weights[k].shape[1])
        row = lax.broadcasted_iota(jnp.int32, shape, 0) + enc * cols
        lane = lax.broadcasted_iota(jnp.int32, shape, 1)
        weights[k][cols:, :] = jnp.where(row == lane, 1.0, 0.0).astype(BF16)

    for tile in range(tiles):
        at = slice(tile * TILE, (tile + 1) * TILE)
        for copy in copies[tile * 5 : tile * 5 + 5]:
            copy.wait()
        back_t = dot(proj[...], held[0][at, :], 1, 1)
        back[:, at] = back_t
        for k in range(4):
            low, high = SPANS[k]
            both = dot(weights[k][...], held[1 + k][at, :], 1, 1)
            pre = both[: high - low]
            cdf = normal_cdf(pre)
            slope = cdf + pre * jnp.exp(-0.5 * pre * pre) * INV_ROOT_TAU
            feature[low:high, at] = (both[high - low :] + pre * cdf).astype(BF16)
            hidden[low:high, at] = (back_t[low:high] * slope).astype(BF16)


def forward(place, gathered, acts, cotangent):
    tokens = cotangent.shape[0]
    vmem = pl.BlockSpec(memory_space=pltpu.VMEM)
    return pl.pallas_call(
        forward_kernel,
        in_specs=[pl.BlockSpec(memory_space=pltpu.SMEM)] + [vmem] * 8
        + [pl.BlockSpec(memory_space=pl.ANY)] * 5,
        out_specs=[vmem] * 3,
        scratch_shapes=[
            pltpu.VMEM((2 * (high - low), a.shape[1]), BF16) for (low, high), a in zip(SPANS, acts)
        ]
        + [pltpu.VMEM((COLS, cotangent.shape[1]), BF16)]
        + [pltpu.VMEM(a.shape, BF16) for a in (cotangent, *acts)]
        + [pltpu.SemaphoreType.DMA((tokens // TILE, 5))],
        out_shape=[
            jax.ShapeDtypeStruct((COLS, tokens), BF16),
            jax.ShapeDtypeStruct((COLS, tokens), BF16),
            jax.ShapeDtypeStruct((COLS, tokens), F32),
        ],
        compiler_params=pltpu.CompilerParams(vmem_limit_bytes=MOST),
        name="forward",
    )(place, *gathered, *acts, cotangent)


def send_kernel(place, *refs):
    out = refs[8]
    for source, ref in enumerate(refs[:8]):
        seq = place[source]
        line = seq // 2
        first = (seq % 2) * 4
        wide = jnp.concatenate([ref[j * WIDE : (j + 1) * WIDE, :] for j in range(3)], axis=1)
        narrow = ref[3 * WIDE : W_ROWS, :]
        for j in range(4):
            out[first + j, line] = jnp.concatenate(
                [wide[:, j * WIDE : (j + 1) * WIDE], narrow[:, j * SMALL : (j + 1) * SMALL]],
                axis=1,
            )


def send_rows(place, gathered):
    return pl.pallas_call(
        send_kernel,
        grid_spec=pltpu.PrefetchScalarGridSpec(
            num_scalar_prefetch=1,
            grid=(1,),
            in_specs=[pl.BlockSpec((W_ROWS, LANES), lambda i, p: (0, 0))] * 8,
            out_specs=pl.BlockSpec((8, 4, WIDE, LANES), lambda i, p: (0, 0, 0, 0)),
        ),
        out_shape=jax.ShapeDtypeStruct((8, 4, WIDE, LANES), BF16),
        compiler_params=pltpu.CompilerParams(vmem_limit_bytes=MOST),
        name="send_rows",
    )(place, *gathered)


def expand_kernel(order, rows, out):
    lane = lax.broadcasted_iota(jnp.int32, (WIDE, LANES), 1)
    zero = jnp.zeros((WIDE, LANES), BF16)
    for group in range(4):
        pieces = []
        for j in range(2):
            block = rows[order[4 + group * 2 + j], 0]
            conv = jnp.where(lane < WIDE, block, zero)
            rest = jnp.where(lane < WIDE, zero, block)
            clip = jnp.concatenate([rest[:SMALL], zero[:SMALL]], axis=1)
            turned = pltpu.roll(rest[SMALL:].astype(F32), SMALL, 1).astype(BF16)
            eva = jnp.concatenate([zero[:SMALL], turned[:SMALL]], axis=1)
            later = pltpu.roll(turned[SMALL:].astype(F32), SMALL, 1).astype(BF16)
            sam = jnp.concatenate([zero[:SMALL], later], axis=1)
            conv = jnp.concatenate([conv, zero], axis=1)
            pieces += [conv, clip, eva, sam]
        both = jnp.concatenate(pieces, axis=0)
        turned = both.astype(F32).T.astype(BF16)
        out[0, :, group * 2 * COLS : (group + 1) * 2 * COLS] = turned[:COLS]


def expand(order, rows):
    return pl.pallas_call(
        expand_kernel,
        grid_spec=pltpu.PrefetchScalarGridSpec(
            num_scalar_prefetch=1,
            grid=(4,),
            in_specs=[pl.BlockSpec((8, 1, WIDE, LANES), lambda i, p: (0, p[i], 0, 0))],
            out_specs=pl.BlockSpec((1, COLS, 8 * COLS), lambda i, p: (i, 0, 0)),
        ),
        out_shape=jax.ShapeDtypeStruct((4, COLS, 8 * COLS), BF16),
        compiler_params=pltpu.CompilerParams(vmem_limit_bytes=VMEM),
        name="expand_rows",
    )(order, rows)


def grads_kernel(order, hidden, feature, *refs):
    sources = refs[:5]
    outs = refs[5:9]
    held = refs[9:14]
    arrived = refs[14]
    copies = []
    for step in range(4):
        for i, (source, target) in enumerate(zip(sources, held)):
            width = target.shape[2]
            copy = pltpu.make_async_copy(
                source.at[:, lanes_of(order[step] * width, width)],
                target.at[step],
                arrived.at[step, i],
            )
            copy.start()
            copies.append(copy)
    for step, out in enumerate(outs):
        for copy in copies[step * 5 : step * 5 + 5]:
            copy.wait()
        wide = dot(hidden[:WIDE, :], held[0][step], 1, 0)
        for j in range(3):
            out[j * WIDE : (j + 1) * WIDE, :] = wide[:, j * LANES : (j + 1) * LANES].astype(BF16)
        row = 3 * WIDE
        for (low, high), ref in zip(SPANS[1:], held[1:4]):
            out[row : row + SMALL, :] = dot(hidden[low:high, :], ref[step], 1, 0).astype(BF16)
            row += SMALL
        proj = dot(feature[...], held[4][step], 1, 0)
        for j in range(5):
            at = W_ROWS + j * COLS
            out[at : at + COLS, :] = proj[:, j * LANES : (j + 1) * LANES].astype(BF16)


def grads(order, hidden, feature, acts, cotangent):
    arrays = (*acts, cotangent)
    vmem = pl.BlockSpec(memory_space=pltpu.VMEM)
    return pl.pallas_call(
        grads_kernel,
        in_specs=[pl.BlockSpec(memory_space=pltpu.SMEM)]
        + [vmem] * 2
        + [pl.BlockSpec(memory_space=pl.ANY)] * 5,
        out_specs=[vmem] * 4,
        out_shape=[jax.ShapeDtypeStruct((ROWS, LANES), BF16)] * 4,
        scratch_shapes=[pltpu.VMEM((4, a.shape[0], a.shape[1] // 8), BF16) for a in arrays]
        + [pltpu.SemaphoreType.DMA((4, 5))],
        compiler_params=pltpu.CompilerParams(vmem_limit_bytes=MOST),
        name="grads",
    )(order, hidden, feature, *arrays)


def away_kernel(*refs):
    total = refs[0][...].astype(F32)
    for ref in refs[1:4]:
        total += ref[...].astype(F32)
    refs[4][...] = total.astype(BF16)


def away_sum(parts):
    return pl.pallas_call(
        away_kernel,
        out_shape=jax.ShapeDtypeStruct((ROWS, LANES), BF16),
        compiler_params=pltpu.CompilerParams(vmem_limit_bytes=MOST),
        name="away_sum",
    )(*parts)


def unpack_kernel(factor, *refs):
    parts = refs[:5]
    wv, wc, we, ws, pv, pc, pe, ps = refs[5:]

    def total(low, high):
        rows = parts[0][low:high].astype(F32)
        for ref in parts[1:]:
            rows += ref[low:high].astype(F32)
        return rows * factor

    for j in range(3):
        wv[:, j * LANES : (j + 1) * LANES] = total(j * WIDE, (j + 1) * WIDE)
    row = 3 * WIDE
    for ref in (wc, we, ws):
        ref[...] = total(row, row + SMALL)
        row += SMALL
    for j in range(5):
        at = W_ROWS + j * COLS
        for ref, (low, high) in zip((pv, pc, pe, ps), SPANS):
            ref[:, j * LANES : (j + 1) * LANES] = total(at + low, at + high)


def unpack(parts, factor):
    sizes = [(WIDE, 384)] + [(SMALL, 128)] * 3 + [(WIDE, 640)] + [(SMALL, 640)] * 3
    return pl.pallas_call(
        lambda *refs: unpack_kernel(factor, *refs),
        out_shape=[jax.ShapeDtypeStruct(size, F32) for size in sizes],
        compiler_params=pltpu.CompilerParams(vmem_limit_bytes=VMEM),
        name="unpack",
    )(*parts)


def partial_kernel(rows, *refs):
    outs, whole = refs[8:12], refs[12]

    @pl.when(pl.program_id(0) == 0)
    def _():
        for j, ref in enumerate(refs[:8]):
            whole[j * COLS : (j + 1) * COLS, :] = ref[...]

    part = dot(rows[0], whole[...], 1, 0).astype(BF16)
    for step, out in enumerate(outs):

        @pl.when(pl.program_id(0) == step)
        def _(out=out):
            out[...] = part


def partial_inputs(rows, hidden):
    tokens = hidden[0].shape[1]
    block = pl.BlockSpec((COLS, tokens), lambda i: (0, 0))
    return pl.pallas_call(
        partial_kernel,
        grid=(4,),
        in_specs=[pl.BlockSpec((1, COLS, 8 * COLS), lambda i: (i, 0, 0))] + [block] * 8,
        out_specs=[block] * 4,
        out_shape=[jax.ShapeDtypeStruct((COLS, tokens), BF16)] * 4,
        scratch_shapes=[pltpu.VMEM((8 * COLS, tokens), BF16)],
        compiler_params=pltpu.CompilerParams(vmem_limit_bytes=VMEM),
        name="partial_inputs",
    )(rows, *hidden)


def finish_kernel(back, *refs):
    for (low, high), out in zip(SPANS, refs[4:]):
        total = refs[0][low:high].astype(F32)
        for ref in refs[1:4]:
            total += ref[low:high].astype(F32)
        out[...] = (back[low:high, :] + total).astype(BF16)


def finish(parts, back):
    tokens = back.shape[1]
    return pl.pallas_call(
        finish_kernel,
        out_shape=[jax.ShapeDtypeStruct((high - low, tokens), BF16) for low, high in SPANS],
        compiler_params=pltpu.CompilerParams(vmem_limit_bytes=VMEM),
        name="finish",
    )(back, *parts)


def body(
    acts_clip,
    acts_convnext,
    acts_eva,
    acts_sam,
    cotangent,
    weight_clip,
    weight_convnext,
    weight_eva,
    weight_sam,
    proj_clip,
    proj_convnext,
    proj_eva,
    proj_sam,
):
    acts = (acts_convnext, acts_clip, acts_eva, acts_sam)
    zh = lax.axis_index("zh")
    y = lax.axis_index("y")
    enc = lax.axis_index(ENC)
    factor = float(8 * cotangent.shape[0]) ** (-0.5)

    def turn(block, shift, axis="y"):
        return lax.ppermute(block, axis, [(i, (i + shift) % 4) for i in range(4)])

    def around(block, axis="y"):
        return [block] + [turn(block, shift, axis) for shift in SHIFTS]

    def turned(blocks, axis="y"):
        return [blocks[0]] + [turn(b, shift, axis) for b, shift in zip(blocks[1:], SHIFTS)]

    own = pack(
        weight_convnext.T,
        weight_clip.T,
        weight_eva.T,
        weight_sam.T,
        proj_convnext.T,
        proj_clip.T,
        proj_eva.T,
        proj_sam.T,
    )
    gathered = around(own) + around(lax.ppermute(own, "zh", SWAP))
    rows_from = [(y - shift) & 3 for shift in (0,) + SHIFTS]
    place = jnp.stack(
        [zh * 4 + r for r in rows_from] + [(1 - zh) * 4 + r for r in rows_from] + [enc]
    ).astype(jnp.int32)

    heads = [(y + shift) & 3 for shift in (0,) + SHIFTS]
    order_away = ((1 - zh) * 4 + jnp.arange(4)).astype(jnp.int32)
    order_near = jnp.stack([zh * 4 + head for head in heads]).astype(jnp.int32)
    zl = lax.axis_index("zl")
    core = lax.axis_index("core")
    x_from = [((lax.axis_index("x") - shift) & 3) * 2 for shift in (0,) + SHIFTS]
    order_rows = jnp.stack(
        [(zl + shift) & 3 for shift in (0,) + SHIFTS]
        + [x + core for x in x_from]
        + [x + 1 - core for x in x_from]
    ).astype(jnp.int32)

    rows = send_rows(place, gathered)
    rows, gathered = lax.optimization_barrier((rows, gathered))
    rows = lax.all_to_all(rows, ("x", "core"), split_axis=0, concat_axis=0, tiled=True)

    hidden, feature, back = forward(place, gathered, acts, cotangent)
    hidden_all = around(hidden, "x")
    hidden_all = hidden_all + [lax.ppermute(block, "core", SWAP) for block in hidden_all]

    away = jnp.stack(grads(order_away, hidden, feature, acts, cotangent))
    away = lax.all_to_all(away, "y", split_axis=0, concat_axis=0, tiled=True)
    other = lax.ppermute(away_sum([away[j] for j in range(4)]), "zh", SWAP)

    parts = partial_inputs(expand(order_rows, rows), hidden_all)
    parts, hidden, feature = lax.optimization_barrier((parts, hidden, feature))
    sums = turned(grads(order_near, hidden, feature, acts, cotangent)) + [other]
    parts = turned(parts, "zl")
    out_v, out_c, out_e, out_s = finish(parts, back)
    wv, wc, we, ws, pv, pc, pe, ps = unpack(sums, factor)
    outs = (out_c, out_v, out_e, out_s, wc, wv, we, ws, pc, pv, pe, ps)
    return tuple(out.T for out in outs)


def solution(mesh):
    split = Mesh(mesh.devices.reshape(4, 4, 2, 2, 4), ("zl", "x", "core", "zh", "y"))
    seq = ("zh", "y")
    whole = P(seq, None)
    tiled = P(seq, ENC)
    return jax.shard_map(
        body,
        mesh=split,
        in_specs=(whole,) * 5 + (tiled,) * 8,
        out_specs=(tiled,) * 12,
        check_vma=False,
    )
```
